32 devices in a mesh: dp: 4 (over y, x), ctx: 2 (over core), head: 4 (over z).
Axes of the slice: x: 2, y: 2, z: 4, core: 2. Of those that a mesh axis runs over, the one named last changes fastest.
Arguments:
- token_values: bfloat16 [4, 1024, 8192], P('dp', 'ctx', 'head'), may hold values from -6 to 6
- gate_values: bfloat16 [4, 1024, 8192], P('dp', 'ctx', 'head'), may hold values from -6 to 6
- state_maps: bfloat16 [4, 1024, 8, 512], P('dp', 'ctx', 'head'), may hold values from -6 to 6
- step_raw: bfloat16 [4, 1024, 128], P('dp', 'ctx', 'head'), may hold values from -6.7 to 2.458448
- log_rate: float32 [128], P('head'), may hold values from -6 to 3
- skip_gain: float32 [128], P('head'), may hold values from 0.5 to 1.5
- conv_values: float32 [4, 8192], P(None, 'head'), may hold values from -3 to 3
- conv_maps: float32 [4, 8, 512], P(None, 'head'), may hold values from -3 to 3
- piece_shift: int32 [32], replicated, may hold values from 0 to 7, as said below
- doc_start: int32 [4, 1024], P('dp', 'ctx'), may hold values 0 or 1
- norm_gain: float32 [8192], P('head'), may hold values from 0.1 to 1.9
- out_weight: bfloat16 [8192, 4096], P('head'), may hold values from -0.0625 to 0.0625
Outputs:
- mixed: bfloat16 [4, 1024, 4096], P('dp', 'ctx', 'head')
The draws below stay inside these ranges and needn't reach their ends.
Inputs may be any that keep to these rules, and one draw needn't show every extreme that they name: `piece_shift`: no value occurs more than 8 times and some value occurs exactly 8 times.
All inputs are finite; a program needn't handle non-finite values. No bound on the sum of `doc_start` on one device may be relied on, other than what follows from the above.
Results may differ from the reference program's by a relative error of at most 0.014.
Values may be sent and summed in bfloat16 or wider, within the bound.
A program may use at most 256 MiB of HBM per device.

```python
import math
import jax
import jax.numpy as jnp
from jax import lax

D = 4096
HEADS = 128
HEAD_DIM = 64
STATE = 256
GROUPS = 8
KERNEL = 4
BLOCK_LEN = 128
PIECES_DEV = 32
TOK_DEV = 512
OWNERS = 8
MOST = 8
BUNDLE_SLOTCOUNT = 1024
INNER = 8192
N_DP = 4


def draw_log_rate(key, part):
    nominal_interval_width = math.log(1.0 + math.exp(-6.0))
    lookup_matrix_lines = jax.random.split(key, 3)
    share = 0.5
    slow = jax.random.uniform(lookup_matrix_lines[0], (HEADS,)) < share
    slow_rate = jax.random.uniform(lookup_matrix_lines[1], (HEADS,), minval=0.25, maxval=0.75) / (BUNDLE_SLOTCOUNT * nominal_interval_width)
    fast_rate = jax.random.uniform(lookup_matrix_lines[2], (HEADS,), minval=0.75, maxval=1.25) / (40.0 * nominal_interval_width)
    return jnp.log(jnp.where(slow, slow_rate, fast_rate)).astype(jnp.float32)


def draw_step_raw(key, part):
    nominal_interval_width = math.log(1.0 + math.exp(-6.0))
    spike_interval_width = 0.95 * BUNDLE_SLOTCOUNT * nominal_interval_width
    spike_amplitude = math.log(math.exp(spike_interval_width) - 1.0)
    lookup_matrix_lines = jax.random.split(key, 2)
    stochastic_perturbation = jax.random.uniform(lookup_matrix_lines[0], (N_DP, BUNDLE_SLOTCOUNT, HEADS), minval=-0.7, maxval=0.7)
    spike_occurrence = jax.random.uniform(lookup_matrix_lines[1], (N_DP, BUNDLE_SLOTCOUNT, 1)) < 2.0 / BUNDLE_SLOTCOUNT
    payload_matrix_lines = jnp.where(spike_occurrence, spike_amplitude, -6.0 + stochastic_perturbation)
    return payload_matrix_lines.astype(jnp.float32).astype(jnp.bfloat16)


def draw_piece_shift(key, part):
    lookup_matrix_lines = jax.random.split(key, 3)
    first = jax.random.randint(lookup_matrix_lines[0], (), 0, OWNERS)
    pool = jax.random.permutation(lookup_matrix_lines[1], OWNERS * MOST) // MOST
    scores = jnp.where(pool == first, 0, 1 + jnp.arange(OWNERS * MOST))
    ordered = pool[jnp.argsort(scores, stable=True)]
    picked = ordered[:PIECES_DEV]
    return jax.random.permutation(lookup_matrix_lines[2], picked).astype(jnp.int32)


def place_ends(values, rng, smallest, top_value):
    dims = values.shape
    place = [jax.random.randint(jax.random.fold_in(rng, axis), (), 0, dims[axis]) for axis in range(len(dims))]
    values = values.at[tuple(place)].set(smallest)
    longest = dims.index(max(dims))
    place[longest] = (place[longest] + 1) % dims[longest]
    return values.at[tuple(place)].set(top_value)


def block_levels(rng, shape, cuts, low, largest):
    def one(dim, parts):
        heights = jax.random.uniform(jax.random.fold_in(jax.random.fold_in(rng, 6), dim), (parts,), jnp.float32, low / len(cuts), largest / len(cuts))
        return jnp.repeat(jnp.exp(heights), shape[dim] // parts).reshape((-1,) + (1,) * (len(shape) - dim - 1))

    level = one(*cuts[0])
    for cut in cuts[1:]:
        level = level * one(*cut)
    return level


def normal_values(stream_key, shape, deviation, bound, cuts=(), kind=jnp.bfloat16):
    values = deviation * jax.random.normal(stream_key, shape, jnp.float32)
    if cuts:
        values = values * block_levels(stream_key, shape, cuts, -0.22, 0.18)
    return jnp.clip(values, -bound, bound).astype(kind)


def setup_inputs(seed: int = 0) -> dict:
    streams_of = jax.random.split(jax.random.key(seed), 13)
    token_values = normal_values(streams_of[0], (N_DP, BUNDLE_SLOTCOUNT, INNER), 1.0, 6.0, ((0, 4), (1, 2), (2, 4)))
    gate_values = normal_values(streams_of[1], (N_DP, BUNDLE_SLOTCOUNT, INNER), 1.0, 6.0, ((0, 4), (1, 2), (2, 4)))
    state_maps = normal_values(streams_of[2], (N_DP, BUNDLE_SLOTCOUNT, GROUPS, 2 * STATE), 1.0, 6.0, ((0, 4), (1, 2), (2, 4)))
    step_raw = draw_step_raw(jax.random.fold_in(streams_of[12], 71), 0)
    log_rate = draw_log_rate(jax.random.fold_in(streams_of[12], 71), 0)
    skip_gain = jnp.clip(0.5 + 1.0 * jax.random.uniform(streams_of[5], (HEADS,), jnp.float32) ** block_levels(streams_of[5], (HEADS,), ((0, 4),), -0.2, 0.2), 0.5, 1.5)
    conv_values = normal_values(streams_of[6], (KERNEL, INNER), KERNEL ** -0.5, 3.0, ((1, 4),), jnp.float32)
    conv_maps = normal_values(streams_of[7], (KERNEL, GROUPS, 2 * STATE), KERNEL ** -0.5, 3.0, ((1, 4),), jnp.float32)
    piece_shift = draw_piece_shift(jax.random.fold_in(streams_of[12], 71), 0)
    doc_start = place_ends((jax.random.randint(streams_of[9], (N_DP, BUNDLE_SLOTCOUNT), 0, BUNDLE_SLOTCOUNT) < 2).astype(jnp.int32), jax.random.fold_in(streams_of[9], 1), 0, 1)
    norm_gain = jnp.clip(1.0 + 0.18 * jax.random.normal(streams_of[10], (INNER,), jnp.float32), 0.1, 1.9)
    out_weight = normal_values(streams_of[11], (INNER, D), INNER ** -0.5, 0.0625, ((0, 4),))
    return {"token_values": token_values, "gate_values": gate_values, "state_maps": state_maps, "step_raw": step_raw, "log_rate": log_rate, "skip_gain": skip_gain, "conv_values": conv_values, "conv_maps": conv_maps, "piece_shift": piece_shift, "doc_start": doc_start, "norm_gain": norm_gain, "out_weight": out_weight}


eps = 1e-05
highest = lax.Precision.HIGHEST

def conv_core(ext_values, weight, free_ext, length):
    tap_count = weight.shape[0]
    summed = jnp.zeros((length,) + ext_values.shape[1:], jnp.float32)
    keeping = jnp.ones((length,), jnp.float32)
    bshape = (length,) + (1,) * (ext_values.ndim - 1)
    for back in range(tap_count):
        if back > 0:
            keeping = keeping * free_ext[tap_count - back:tap_count - back + length]
        sample = ext_values[tap_count - 1 - back:tap_count - 1 - back + length].astype(jnp.float32)
        summed = summed + weight[tap_count - 1 - back] * sample * keeping.reshape(bshape)
    return jax.nn.silu(summed).astype(jnp.bfloat16)

def conv_silu(payload_matrix_lines, weight, free_flags):
    tap_count = weight.shape[0]
    padded = jnp.concatenate([jnp.zeros((tap_count - 1,) + payload_matrix_lines.shape[1:], payload_matrix_lines.dtype), payload_matrix_lines])
    free_ext = jnp.concatenate([jnp.ones((tap_count - 1,), jnp.float32), free_flags])
    return conv_core(padded, weight, free_ext, payload_matrix_lines.shape[0])

def mix_group(payload_matrix_lines, gates, maps, steps, rates, skips, conv_v, conv_m, starts, gains):
    length = payload_matrix_lines.shape[0]
    heads_here = rates.shape[0]
    width = payload_matrix_lines.shape[1] // heads_here
    state = maps.shape[1] // 2
    blocks = length // BLOCK_LEN
    free_flags = 1.0 - starts.astype(jnp.float32)
    x_conv = conv_silu(payload_matrix_lines, conv_v, free_flags)
    map_conv = conv_silu(maps, conv_m, free_flags)
    step_dt = jax.nn.softplus(steps.astype(jnp.float32))
    log_decay = step_dt * (-jnp.exp(rates))[None, :]
    cum_t = jnp.cumsum(log_decay.reshape(blocks, BLOCK_LEN, heads_here), axis=1).transpose(0, 2, 1)
    dt_t = step_dt.reshape(blocks, BLOCK_LEN, heads_here).transpose(0, 2, 1)
    segment = jnp.cumsum(starts.reshape(blocks, BLOCK_LEN), axis=1)
    x_blocks = x_conv.reshape(blocks, BLOCK_LEN, heads_here, width).astype(jnp.float32)
    b_blocks = map_conv[:, :state].reshape(blocks, BLOCK_LEN, state).astype(jnp.float32)
    c_blocks = map_conv[:, state:].reshape(blocks, BLOCK_LEN, state).astype(jnp.float32)
    scores = jnp.einsum('bqn,bsn->bqs', c_blocks, b_blocks, precision=highest)
    later = jnp.arange(BLOCK_LEN)[:, None] >= jnp.arange(BLOCK_LEN)[None, :]
    allowed = later[None] & (segment[:, :, None] == segment[:, None, :])
    spread = cum_t[:, :, :, None] - cum_t[:, :, None, :]
    decay = jnp.exp(jnp.where(allowed[:, None], spread, -jnp.inf))
    weights = (decay * scores[:, None] * dt_t[:, :, None, :]).astype(jnp.bfloat16)
    y_diag = jnp.einsum('bhts,bshp->bthp', weights.astype(jnp.float32), x_blocks, precision=highest)
    same_end = (segment == segment[:, -1:]).astype(jnp.float32)
    carry_coef = jnp.exp(cum_t[:, :, -1:] - cum_t) * dt_t * same_end[:, None, :]
    x_weighted = (x_blocks * carry_coef.transpose(0, 2, 1)[..., None]).astype(jnp.bfloat16)
    block_states = jnp.einsum('bshp,bsn->bhpn', x_weighted.astype(jnp.float32), b_blocks, precision=highest)
    block_gates = jnp.exp(cum_t[:, :, -1]) * (segment[:, -1] == 0).astype(jnp.float32)[:, None]

    def advance(summed, item):
        gate_now, state_now = item
        return (gate_now[:, None, None] * summed + state_now, summed)
    unused, entering = lax.scan(advance, jnp.zeros((heads_here, width, state), jnp.float32), (block_gates, block_states))
    entering = entering.astype(jnp.bfloat16).astype(jnp.float32)
    y_off = jnp.einsum('bqn,bhpn->bqhp', c_blocks, entering, precision=highest)
    reach = (jnp.exp(cum_t) * (segment == 0).astype(jnp.float32)[:, None, :]).transpose(0, 2, 1)[..., None]
    mixed_y = y_diag + y_off * reach + skips[None, None, :, None] * x_blocks
    gated = mixed_y * jax.nn.silu(gates.astype(jnp.float32).reshape(blocks, BLOCK_LEN, heads_here, width))
    power = lax.optimization_barrier(jnp.mean(gated * gated, axis=(2, 3), keepdims=True))
    normed = gated * lax.rsqrt(power + eps) * gains.reshape(heads_here, width)
    return normed.astype(jnp.bfloat16).reshape(length, heads_here * width)

def reference(token_values, gate_values, state_maps, step_raw, log_rate, skip_gain, conv_values, conv_maps, piece_shift, doc_start, norm_gain, out_weight):
    source = (jnp.arange(OWNERS, dtype=jnp.int32)[:, None] - piece_shift[None, :]) % OWNERS
    slot_ids = jnp.arange(PIECES_DEV, dtype=jnp.int32)[None, :]

    def route(array):
        pieces = array.reshape((OWNERS, PIECES_DEV, TOK_DEV // PIECES_DEV) + array.shape[2:])
        return pieces[source, slot_ids].reshape(array.shape)
    per_group = HEADS // GROUPS
    inner_group = per_group * HEAD_DIM
    payload_matrix_lines = route(token_values).reshape(N_DP, BUNDLE_SLOTCOUNT, GROUPS, inner_group)
    gates = route(gate_values).reshape(N_DP, BUNDLE_SLOTCOUNT, GROUPS, inner_group)
    maps = route(state_maps)
    steps = route(step_raw).reshape(N_DP, BUNDLE_SLOTCOUNT, GROUPS, per_group)
    rates = log_rate.reshape(GROUPS, per_group)
    skips = skip_gain.reshape(GROUPS, per_group)
    conv_v = conv_values.reshape(KERNEL, GROUPS, inner_group)
    gains = norm_gain.reshape(GROUPS, inner_group)

    def one_item(index):
        pack = index // GROUPS
        group = index % GROUPS
        return mix_group(payload_matrix_lines[pack, :, group], gates[pack, :, group], maps[pack, :, group], steps[pack, :, group], rates[group], skips[group], conv_v[:, group], conv_maps[:, group], doc_start[pack], gains[group])
    normed = lax.map(one_item, jnp.arange(N_DP * GROUPS, dtype=jnp.int32))
    normed = normed.reshape(N_DP, GROUPS, BUNDLE_SLOTCOUNT, inner_group).transpose(0, 2, 1, 3).reshape(N_DP, BUNDLE_SLOTCOUNT, HEADS * HEAD_DIM)

    def project(block_rows):
        return jnp.dot(block_rows, out_weight, preferred_element_type=jnp.float32).astype(jnp.bfloat16)
    return lax.map(project, normed)
```

```python
import functools

import jax
import jax.numpy as jnp
from jax import lax
from jax.experimental import pallas as pl
from jax.experimental.pallas import tpu as pltpu
from jax.sharding import PartitionSpec as P

SPAN = 128
eps = 1e-05
F32 = jnp.float32
BF16 = jnp.bfloat16


def silu(u):
    return u * (1.0 / (1.0 + jnp.exp(-u)))


def spread_heads(coef, expand):
    high = coef.astype(BF16)
    low = (coef - high.astype(F32)).astype(BF16)
    return jnp.dot(high, expand, preferred_element_type=F32) + jnp.dot(
        low, expand, preferred_element_type=F32
    )


def conv_cols(buf, cols, taps, marks):
    summed = taps[3:4, :] * buf[8 : 8 + SPAN, cols]
    for back in range(1, 4):
        keep = marks[:, 2 + back : 3 + back]
        summed = summed + (taps[3 - back : 4 - back, :] * buf[8 - back : 8 - back + SPAN, cols]) * keep
    return silu(summed).astype(BF16)


def scan_kernel(pieces, groups, heads, state, width, index_ref, *refs):
    x_refs = refs[:pieces]
    m_refs = refs[pieces : 2 * pieces]
    (rim_x, rim_m, taps_x, taps_m, marks_ref, segrow_ref, cum_ref, rev_ref, carry_ref, reach_ref,
     gate_ref, skip_ref, expand_ref, y_ref, c_ref, slab_ref, xbuf, mbuf, carried) = refs[2 * pieces :]
    block = pl.program_id(0)
    prow = SPAN // pieces
    inner = xbuf.shape[1]
    maps = mbuf.shape[1]

    @pl.when(block == 0)
    def _():
        xbuf[0:8, :] = rim_x[prow - 8 : prow, :].astype(F32)
        mbuf[0:8, :] = rim_m[prow - 8 : prow, :maps].astype(F32)
        carried[...] = jnp.zeros_like(carried)

    @pl.when(block > 0)
    def _():
        xbuf[0:8, :] = xbuf[SPAN : SPAN + 8, :]
        mbuf[0:8, :] = mbuf[SPAN : SPAN + 8, :]

    for k in range(pieces):
        xbuf[8 + k * prow : 8 + (k + 1) * prow, :] = x_refs[k][0].astype(F32)
        mbuf[8 + k * prow : 8 + (k + 1) * prow, :] = m_refs[k][0].astype(F32)
    marks = marks_ref[...]
    seg_t = marks[:, 0:1]
    ti = lax.broadcasted_iota(jnp.int32, (SPAN, SPAN), 0)
    si = lax.broadcasted_iota(jnp.int32, (SPAN, SPAN), 1)
    allowed = (ti >= si) & (seg_t == segrow_ref[0])
    bias = jnp.where(allowed, 0.0, -1e30)
    left = lax.broadcasted_iota(jnp.int32, (SPAN, 2 * width), 1) < width
    cum = cum_ref[...]
    rev = rev_ref[0]
    carry = carry_ref[...]
    reach = reach_ref[...]
    per_group = heads // groups
    for g in range(groups):
        parts = []
        for q in range(2 * state // 128):
            cols = slice(g * 2 * state + q * 128, g * 2 * state + (q + 1) * 128)
            parts.append(conv_cols(mbuf, cols, taps_m[:, cols], marks))
        half = len(parts) // 2
        b_g = jnp.concatenate(parts[:half], axis=1)
        c_g = jnp.concatenate(parts[half:], axis=1)
        c_ref[:, g * state : (g + 1) * state] = c_g
        scores = lax.dot_general(c_g, b_g, (((1,), (1,)), ((), ())), preferred_element_type=F32)
        for p in range(per_group // 2):
            h = g * per_group + 2 * p
            cols = slice(h * width, (h + 2) * width)
            xc = conv_cols(xbuf, cols, taps_x[:, cols], marks)
            weights = []
            for k in (h, h + 1):
                decay = jnp.exp((cum[:, k : k + 1] + rev[k : k + 1, :]) + bias)
                weights.append((decay * scores).astype(BF16))
            zero = jnp.zeros_like(xc)
            both = jnp.concatenate([jnp.where(left, xc, zero), jnp.where(left, zero, xc)], axis=0)
            y = jnp.dot(jnp.concatenate(weights, axis=1), both, preferred_element_type=F32)
            expand = expand_ref[:, cols]
            prior = carried[:, cols]
            off = jnp.dot(c_g, prior.astype(BF16), preferred_element_type=F32)
            xf = xc.astype(F32)
            y_ref[:, cols] = y + off * spread_heads(reach, expand) + skip_ref[:, cols] * xf
            xw = (xf * spread_heads(carry, expand)).astype(BF16)
            added = lax.dot_general(b_g, xw, (((0,), (0,)), ((), ())), preferred_element_type=F32)
            carried[:, cols] = gate_ref[0, :, cols] * prior + added

    @pl.when(block == pl.num_programs(0) - 1)
    def _():
        slab_ref[...] = carried[...].astype(BF16)


def gate_kernel(pieces, groups, heads, state, width, index_ref, *refs):
    z_refs = refs[:pieces]
    y_ref, c_ref, coef_ref, arriving_ref, expand_ref, gain_ref, out_ref, gated, zbuf = refs[pieces:]
    prow = SPAN // pieces
    for k in range(pieces):
        zbuf[k * prow : (k + 1) * prow, :] = z_refs[k][0]
    coef = coef_ref[...]
    inner = heads * width
    size = inner // groups
    for g in range(groups):
        c_g = c_ref[:, g * state : (g + 1) * state]
        total = jnp.zeros((SPAN, 128), F32)
        for q in range(size // 128):
            cols = slice(g * size + q * 128, g * size + (q + 1) * 128)
            off = jnp.dot(c_g, arriving_ref[:, cols], preferred_element_type=F32)
            y = y_ref[:, cols] + off * spread_heads(coef, expand_ref[:, cols])
            value = y * silu(zbuf[:, cols].astype(F32))
            gated[:, q * 128 : (q + 1) * 128] = value
            total = total + value * value
        scale = lax.rsqrt(jnp.sum(total, axis=1, keepdims=True) * (1.0 / size) + eps)
        for q in range(size // 128):
            cols = slice(g * size + q * 128, g * size + (q + 1) * 128)
            out_ref[:, cols] = (
                gated[:, q * 128 : (q + 1) * 128] * scale * gain_ref[:, cols]
            ).astype(BF16)


def passed_along(block, axis, distance):
    devices = range(lax.axis_size(axis))
    route = [(i - distance, i) for i in devices if i - distance in devices]
    return lax.ppermute(block, axis, route)


def body(token_values, gate_values, state_maps, step_raw, log_rate, skip_gain, conv_values, conv_maps,
         piece_shift, doc_start, norm_gain, out_weight):
    owners = lax.axis_size(("dp", "ctx"))
    myself = lax.axis_index(("dp", "ctx"))
    slots = piece_shift.shape[0]
    rows = token_values.shape[1]
    prow = rows // slots
    most = 2 * slots // owners
    inner = token_values.shape[2]
    heads = log_rate.shape[0]
    groups = state_maps.shape[2]
    state = state_maps.shape[3] // 2
    maps = groups * 2 * state
    width = inner // heads
    blocks = rows // SPAN
    pieces = SPAN // prow

    slot_ids = jnp.arange(slots, dtype=jnp.int32)
    matching = piece_shift[:, None] == piece_shift[None, :]
    ranking = jnp.sum((matching & (slot_ids[None, :] < slot_ids[:, None])).astype(jnp.int32), axis=1)
    offsets = (jnp.arange(owners, dtype=jnp.int32) - myself) % owners
    chosen = (piece_shift[None, None, :] == offsets[:, None, None]) & (
        ranking[None, None, :] == jnp.arange(most, dtype=jnp.int32)[None, :, None]
    )
    send_slot = jnp.sum(chosen.astype(jnp.int32) * slot_ids[None, None, :], axis=2)
    source = (myself - piece_shift) % owners
    index = source * most + ranking

    def exchange(local):
        cut = local.reshape(slots, prow, local.shape[-1])
        got = lax.all_to_all(cut[send_slot], ("dp", "ctx"), split_axis=0, concat_axis=0, tiled=True)
        return got.reshape(owners * most, prow, local.shape[-1])

    steps = jnp.pad(step_raw[0], ((0, 0), (0, (-heads) % 128)))
    m_got = exchange(jnp.concatenate([state_maps[0].reshape(rows, maps), steps], axis=1))
    x_got = exchange(token_values[0])
    z_got = exchange(gate_values[0])

    flags = doc_start[0].astype(F32)
    tail = passed_along(flags[rows - 3 :], "ctx", 1)
    free = 1.0 - jnp.concatenate([tail, flags])
    k1 = free[3:]
    k2 = k1 * free[2 : 2 + rows]
    k3 = k2 * free[1 : 1 + rows]
    segment = jnp.cumsum(flags.reshape(blocks, SPAN), axis=1)
    same_end = (segment == segment[:, -1:]).astype(F32)
    first = (segment == 0).astype(F32)
    nil = jnp.zeros((rows,), F32)
    marks = jnp.stack(
        [segment.reshape(rows), same_end.reshape(rows), first.reshape(rows), k1, k2, k3, nil, nil], axis=1
    )

    dt_raw = m_got[index][:, :, maps : maps + heads].reshape(rows, heads)
    dt = jax.nn.softplus(dt_raw.astype(F32)).reshape(blocks, SPAN, heads)
    cum = jnp.cumsum(dt * (-jnp.exp(log_rate)), axis=1)
    rev = (jnp.log(dt) - cum).transpose(0, 2, 1)
    last = cum[:, -1:]
    carry = jnp.exp(last - cum) * dt * same_end[:, :, None]
    reach = jnp.exp(cum) * first[:, :, None]
    gates = jnp.exp(cum[:, -1]) * first[:, -1:]
    before = [jnp.ones((heads,), F32)]
    for b in range(blocks):
        before.append(before[-1] * gates[b])
    coef = reach * jnp.stack(before[:blocks])[:, None, :]
    gate_rows = jnp.repeat(gates, width, axis=1)[:, None, :]
    expand = (
        jnp.arange(heads)[:, None] == jnp.arange(inner)[None, :] // width
    ).astype(BF16)

    rim_m, rim_x = passed_along(
        (m_got[index[slots - 1]], x_got[index[slots - 1]]), "ctx", 1
    )

    def piece_specs(cols):
        return [
            pl.BlockSpec((1, prow, cols), functools.partial(lambda k, b, i: (i[b * pieces + k], 0, 0), k))
            for k in range(pieces)
        ]

    def whole(shape):
        return pl.BlockSpec(shape, lambda b, i: (0,) * len(shape))

    def by_block(cols):
        return pl.BlockSpec((SPAN, cols), lambda b, i: (b, 0))

    lim = 48 * 1024 * 1024
    y_part, c_all, slab = pl.pallas_call(
        functools.partial(scan_kernel, pieces, groups, heads, state, width),
        grid_spec=pltpu.PrefetchScalarGridSpec(
            num_scalar_prefetch=1,
            grid=(blocks,),
            in_specs=piece_specs(inner)
            + piece_specs(maps)
            + [
                whole((prow, inner)),
                whole(rim_m.shape),
                whole((4, inner)),
                whole((4, maps)),
                by_block(8),
                pl.BlockSpec((1, 1, SPAN), lambda b, i: (b, 0, 0)),
                by_block(heads),
                pl.BlockSpec((1, heads, SPAN), lambda b, i: (b, 0, 0)),
                by_block(heads),
                by_block(heads),
                pl.BlockSpec((1, 1, inner), lambda b, i: (b, 0, 0)),
                whole((1, inner)),
                whole((heads, inner)),
            ],
            out_specs=[by_block(inner), by_block(groups * state), whole((state, inner))],
            scratch_shapes=[
                pltpu.VMEM((SPAN + 8, inner), F32),
                pltpu.VMEM((SPAN + 8, maps), F32),
                pltpu.VMEM((state, inner), F32),
            ],
        ),
        out_shape=[
            jax.ShapeDtypeStruct((rows, inner), F32),
            jax.ShapeDtypeStruct((rows, groups * state), BF16),
            jax.ShapeDtypeStruct((state, inner), BF16),
        ],
        compiler_params=pltpu.CompilerParams(vmem_limit_bytes=lim),
        cost_estimate=pl.CostEstimate(flops=4_000_000_000, bytes_accessed=12_000_000, transcendentals=4_000_000),
        name="scan",
    )(
        index,
        *([x_got] * pieces),
        *([m_got] * pieces),
        rim_x,
        rim_m,
        conv_values,
        conv_maps.reshape(4, maps),
        marks,
        segment[:, None, :],
        cum.reshape(rows, heads),
        rev,
        carry.reshape(rows, heads),
        reach.reshape(rows, heads),
        gate_rows,
        jnp.repeat(skip_gain, width)[None, :],
        expand,
    )

    if lax.axis_size("ctx") == 2:
        arriving = passed_along(slab, "ctx", 1)
    else:
        slabs = lax.all_gather(slab, "ctx")
        factors = lax.all_gather(jnp.repeat(before[blocks], width), "ctx")

        def one(turn, total):
            return (
                lax.dynamic_index_in_dim(factors, turn, 0, False)[None, :] * total
                + lax.dynamic_index_in_dim(slabs, turn, 0, False).astype(F32)
            )

        arriving = lax.fori_loop(0, lax.axis_index("ctx"), one, jnp.zeros(slab.shape, F32)).astype(BF16)

    normed = pl.pallas_call(
        functools.partial(gate_kernel, pieces, groups, heads, state, width),
        grid_spec=pltpu.PrefetchScalarGridSpec(
            num_scalar_prefetch=1,
            grid=(blocks,),
            in_specs=piece_specs(inner)
            + [
                by_block(inner),
                by_block(groups * state),
                by_block(heads),
                whole((state, inner)),
                whole((heads, inner)),
                whole((1, inner)),
            ],
            out_specs=by_block(inner),
            scratch_shapes=[pltpu.VMEM((SPAN, inner // groups), F32), pltpu.VMEM((SPAN, inner), BF16)],
        ),
        out_shape=jax.ShapeDtypeStruct((rows, inner), BF16),
        compiler_params=pltpu.CompilerParams(vmem_limit_bytes=lim),
        cost_estimate=pl.CostEstimate(flops=1_000_000_000, bytes_accessed=10_000_000, transcendentals=1_000_000),
        name="gating",
    )(
        index,
        *([z_got] * pieces),
        y_part,
        c_all,
        coef.reshape(rows, heads),
        arriving,
        expand,
        norm_gain[None, :],
    )
    partial_value = jnp.dot(normed, out_weight, preferred_element_type=F32)
    result = lax.psum_scatter(partial_value.astype(BF16), "head", scatter_dimension=1, tiled=True)
    return result[None]


def solution(mesh):
    return jax.shard_map(
        body,
        mesh=mesh,
        in_specs=(
            P("dp", "ctx", "head"),
            P("dp", "ctx", "head"),
            P("dp", "ctx", "head", None),
            P("dp", "ctx", "head"),
            P("head"),
            P("head"),
            P(None, "head"),
            P(None, "head", None),
            P(),
            P("dp", "ctx"),
            P("head"),
            P("head", None),
        ),
        out_specs=P("dp", "ctx", "head"),
        check_vma=False,
    )
```

```python
import functools

import jax
import jax.numpy as jnp
from jax import lax
from jax.experimental import pallas as pl
from jax.experimental.pallas import tpu as pltpu
from jax.sharding import PartitionSpec as P

SPAN = 128
eps = 1e-05
F32 = jnp.float32
BF16 = jnp.bfloat16


def silu(u):
    return u * (1.0 / (1.0 + jnp.exp(-u)))


def spread_heads(coef, expand):
    high = coef.astype(BF16)
    low = (coef - high.astype(F32)).astype(BF16)
    return jnp.dot(high, expand, preferred_element_type=F32) + jnp.dot(
        low, expand, preferred_element_type=F32
    )


def conv_cols(buf, cols, taps, marks):
    summed = taps[3:4, :] * buf[8 : 8 + SPAN, cols]
    for back in range(1, 4):
        keep = marks[:, 2 + back : 3 + back]
        summed = summed + (taps[3 - back : 4 - back, :] * buf[8 - back : 8 - back + SPAN, cols]) * keep
    return silu(summed).astype(BF16)


def scan_kernel(pieces, groups, heads, state, width, index_ref, *refs):
    x_refs = refs[:pieces]
    m_refs = refs[pieces : 2 * pieces]
    (rim_x, rim_m, taps_x, taps_m, marks_ref, segrow_ref, cum_ref, rev_ref, carry_ref, reach_ref,
     gate_ref, skip_ref, expand_ref, y_ref, c_ref, slab_ref, xbuf, mbuf, carried) = refs[2 * pieces :]
    block = pl.program_id(0)
    prow = SPAN // pieces
    inner = xbuf.shape[1]
    maps = mbuf.shape[1]

    @pl.when(block == 0)
    def _():
        xbuf[0:8, :] = rim_x[prow - 8 : prow, :].astype(F32)
        mbuf[0:8, :] = rim_m[prow - 8 : prow, :maps].astype(F32)
        carried[...] = jnp.zeros_like(carried)

    @pl.when(block > 0)
    def _():
        xbuf[0:8, :] = xbuf[SPAN : SPAN + 8, :]
        mbuf[0:8, :] = mbuf[SPAN : SPAN + 8, :]

    for k in range(pieces):
        xbuf[8 + k * prow : 8 + (k + 1) * prow, :] = x_refs[k][0].astype(F32)
        mbuf[8 + k * prow : 8 + (k + 1) * prow, :] = m_refs[k][0].astype(F32)
    marks = marks_ref[...]
    seg_t = marks[:, 0:1]
    ti = lax.broadcasted_iota(jnp.int32, (SPAN, SPAN), 0)
    si = lax.broadcasted_iota(jnp.int32, (SPAN, SPAN), 1)
    allowed = (ti >= si) & (seg_t == segrow_ref[0])
    bias = jnp.where(allowed, 0.0, -1e30)
    left = lax.broadcasted_iota(jnp.int32, (SPAN, 2 * width), 1) < width
    cum = cum_ref[...]
    rev = rev_ref[0]
    carry = carry_ref[...]
    reach = reach_ref[...]
    per_group = heads // groups
    for g in range(groups):
        parts = []
        for q in range(2 * state // 128):
            cols = slice(g * 2 * state + q * 128, g * 2 * state + (q + 1) * 128)
            parts.append(conv_cols(mbuf, cols, taps_m[:, cols], marks))
        half = len(parts) // 2
        b_g = jnp.concatenate(parts[:half], axis=1)
        c_g = jnp.concatenate(parts[half:], axis=1)
        c_ref[:, g * state : (g + 1) * state] = c_g
        scores = lax.dot_general(c_g, b_g, (((1,), (1,)), ((), ())), preferred_element_type=F32)
        for p in range(per_group // 2):
            h = g * per_group + 2 * p
            cols = slice(h * width, (h + 2) * width)
            xc = conv_cols(xbuf, cols, taps_x[:, cols], marks)
            weights = []
            for k in (h, h + 1):
                decay = jnp.exp((cum[:, k : k + 1] + rev[k : k + 1, :]) + bias)
                weights.append((decay * scores).astype(BF16))
            zero = jnp.zeros_like(xc)
            both = jnp.concatenate([jnp.where(left, xc, zero), jnp.where(left, zero, xc)], axis=0)
            y = jnp.dot(jnp.concatenate(weights, axis=1), both, preferred_element_type=F32)
            expand = expand_ref[:, cols]
            prior = carried[:, cols]
            off = jnp.dot(c_g, prior.astype(BF16), preferred_element_type=F32)
            xf = xc.astype(F32)
            y_ref[:, cols] = y + off * spread_heads(reach, expand) + skip_ref[:, cols] * xf
            xw = (xf * spread_heads(carry, expand)).astype(BF16)
            added = lax.dot_general(b_g, xw, (((0,), (0,)), ((), ())), preferred_element_type=F32)
            carried[:, cols] = gate_ref[0, :, cols] * prior + added

    @pl.when(block == pl.num_programs(0) - 1)
    def _():
        slab_ref[...] = carried[...].astype(BF16)


def gate_kernel(pieces, groups, heads, state, width, index_ref, *refs):
    z_refs = refs[:pieces]
    y_ref, c_ref, coef_ref, arriving_ref, expand_ref, gain_ref, out_ref, gated, zbuf = refs[pieces:]
    prow = SPAN // pieces
    for k in range(pieces):
        zbuf[k * prow : (k + 1) * prow, :] = z_refs[k][0]
    coef = coef_ref[...]
    inner = heads * width
    size = inner // groups
    for g in range(groups):
        c_g = c_ref[:, g * state : (g + 1) * state]
        total = jnp.zeros((SPAN, 128), F32)
        for q in range(size // 128):
            cols = slice(g * size + q * 128, g * size + (q + 1) * 128)
            off = jnp.dot(c_g, arriving_ref[:, cols], preferred_element_type=F32)
            y = y_ref[:, cols] + off * spread_heads(coef, expand_ref[:, cols])
            value = y * silu(zbuf[:, cols].astype(F32))
            gated[:, q * 128 : (q + 1) * 128] = value
            total = total + value * value
        scale = lax.rsqrt(jnp.sum(total, axis=1, keepdims=True) * (1.0 / size) + eps)
        for q in range(size // 128):
            cols = slice(g * size + q * 128, g * size + (q + 1) * 128)
            out_ref[:, cols] = (
                gated[:, q * 128 : (q + 1) * 128] * scale * gain_ref[:, cols]
            ).astype(BF16)


def passed_along(block, axis, distance):
    devices = range(lax.axis_size(axis))
    route = [(i - distance, i) for i in devices if i - distance in devices]
    return lax.ppermute(block, axis, route)


def body(token_values, gate_values, state_maps, step_raw, log_rate, skip_gain, conv_values, conv_maps,
         piece_shift, doc_start, norm_gain, out_weight):
    owners = lax.axis_size(("dp", "ctx"))
    myself = lax.axis_index(("dp", "ctx"))
    slots = piece_shift.shape[0]
    rows = token_values.shape[1]
    prow = rows // slots
    most = 2 * slots // owners
    inner = token_values.shape[2]
    heads = log_rate.shape[0]
    groups = state_maps.shape[2]
    state = state_maps.shape[3] // 2
    maps = groups * 2 * state
    width = inner // heads
    blocks = rows // SPAN
    pieces = SPAN // prow

    slot_ids = jnp.arange(slots, dtype=jnp.int32)
    matching = piece_shift[:, None] == piece_shift[None, :]
    ranking = jnp.sum((matching & (slot_ids[None, :] < slot_ids[:, None])).astype(jnp.int32), axis=1)
    base = most // 2 if owners <= 8 else most
    offsets = (jnp.arange(owners, dtype=jnp.int32) - myself) % owners
    chosen = (piece_shift[None, None, :] == offsets[:, None, None]) & (
        ranking[None, None, :] == jnp.arange(base, dtype=jnp.int32)[None, :, None]
    )
    send_slot = jnp.sum(chosen.astype(jnp.int32) * slot_ids[None, None, :], axis=2)
    source = (myself - piece_shift) % owners
    index = source * base + ranking

    def exchange(cut):
        got = lax.all_to_all(cut[send_slot], ("dp", "ctx"), split_axis=0, concat_axis=0, tiled=True)
        return got.reshape((owners * base,) + cut.shape[1:])

    steps = jnp.pad(step_raw[0], ((0, 0), (0, (-heads) % 128)))
    m_cut = jnp.concatenate([state_maps[0].reshape(rows, maps), steps], axis=1).reshape(slots, prow, -1)
    x_cut = token_values[0].reshape(slots, prow, inner)
    z_cut = gate_values[0].reshape(slots, prow, inner)
    cuts = (m_cut, x_cut, z_cut)
    if base < most:
        shifts = jnp.arange(owners, dtype=jnp.int32)
        counts = jnp.sum((piece_shift[None, :] == shifts[:, None]).astype(jnp.int32), axis=1)
        over = (counts > base).astype(jnp.int32)
        place = jnp.sum(over[None, :] * (shifts[None, :] < shifts[:, None]), axis=1)
        spare = slots // (base + 1)
        nth = over[None, :] * (place[None, :] == jnp.arange(spare)[:, None])
        shift_of = jnp.sum(nth * shifts[None, :], axis=1)
        surplus = jnp.sum(nth * (counts - base)[None, :], axis=1)
        late = (piece_shift[None, None, :] == shift_of[:, None, None]) & (
            ranking[None, None, :] == base + jnp.arange(most - base, dtype=jnp.int32)[None, :, None]
        )
        late_slot = jnp.sum(late.astype(jnp.int32) * slot_ids[None, None, :], axis=2)
        mine = jnp.sum((piece_shift[:, None] == shifts[None, :]) * place[None, :], axis=1)
        index = jnp.where(
            ranking < base, index, owners * base + mine * (most - base) + ranking - base
        )

        def moving(shift, number):
            def move(ids, cuts):
                out = []
                for cut in cuts:
                    part = cut[ids[:number]]
                    if shift:
                        part = lax.ppermute(
                            part, ("dp", "ctx"), [(t, (t + shift) % owners) for t in range(owners)]
                        )
                    out.append(jnp.pad(part, ((0, most - base - number), (0, 0), (0, 0))))
                return tuple(out)

            return move

        moves = [moving(s, n) for s in range(owners) for n in range(1, most - base + 1)]

        def one_shift(turn, held):
            which = shift_of[turn] * (most - base) + surplus[turn] - 1
            parts = lax.switch(which, moves, late_slot[turn], cuts)
            return tuple(
                lax.dynamic_update_slice_in_dim(h, p, turn * (most - base), 0)
                for h, p in zip(held, parts)
            )

        held = tuple(jnp.zeros((spare * (most - base),) + cut.shape[1:], cut.dtype) for cut in cuts)
        held = lax.fori_loop(0, jnp.sum(over), one_shift, held)
        m_got, x_got, z_got = (
            jnp.concatenate([exchange(cut), extra]) for cut, extra in zip(cuts, held)
        )
    else:
        m_got, x_got, z_got = (exchange(cut) for cut in cuts)

    flags = doc_start[0].astype(F32)
    tail = passed_along(flags[rows - 3 :], "ctx", 1)
    free = 1.0 - jnp.concatenate([tail, flags])
    k1 = free[3:]
    k2 = k1 * free[2 : 2 + rows]
    k3 = k2 * free[1 : 1 + rows]
    segment = jnp.cumsum(flags.reshape(blocks, SPAN), axis=1)
    same_end = (segment == segment[:, -1:]).astype(F32)
    first = (segment == 0).astype(F32)
    nil = jnp.zeros((rows,), F32)
    marks = jnp.stack(
        [segment.reshape(rows), same_end.reshape(rows), first.reshape(rows), k1, k2, k3, nil, nil], axis=1
    )

    dt_raw = m_got[:, :, maps : maps + heads][index].reshape(rows, heads)
    dt = jax.nn.softplus(dt_raw.astype(F32)).reshape(blocks, SPAN, heads)
    cum = jnp.cumsum(dt * (-jnp.exp(log_rate)), axis=1)
    rev = (jnp.log(dt) - cum).transpose(0, 2, 1)
    last = cum[:, -1:]
    carry = jnp.exp(last - cum) * dt * same_end[:, :, None]
    reach = jnp.exp(cum) * first[:, :, None]
    gates = jnp.exp(cum[:, -1]) * first[:, -1:]
    before = [jnp.ones((heads,), F32)]
    for b in range(blocks):
        before.append(before[-1] * gates[b])
    coef = reach * jnp.stack(before[:blocks])[:, None, :]
    gate_rows = jnp.repeat(gates, width, axis=1)[:, None, :]
    expand = (
        jnp.arange(heads)[:, None] == jnp.arange(inner)[None, :] // width
    ).astype(BF16)

    rim_m, rim_x = passed_along(
        (m_got[index[slots - 1]], x_got[index[slots - 1]]), "ctx", 1
    )

    def piece_specs(cols):
        return [
            pl.BlockSpec((1, prow, cols), functools.partial(lambda k, b, i: (i[b * pieces + k], 0, 0), k))
            for k in range(pieces)
        ]

    def whole(shape):
        return pl.BlockSpec(shape, lambda b, i: (0,) * len(shape))

    def by_block(cols):
        return pl.BlockSpec((SPAN, cols), lambda b, i: (b, 0))

    lim = 48 * 1024 * 1024
    y_part, c_all, slab = pl.pallas_call(
        functools.partial(scan_kernel, pieces, groups, heads, state, width),
        grid_spec=pltpu.PrefetchScalarGridSpec(
            num_scalar_prefetch=1,
            grid=(blocks,),
            in_specs=piece_specs(inner)
            + piece_specs(maps)
            + [
                whole((prow, inner)),
                whole(rim_m.shape),
                whole((4, inner)),
                whole((4, maps)),
                by_block(8),
                pl.BlockSpec((1, 1, SPAN), lambda b, i: (b, 0, 0)),
                by_block(heads),
                pl.BlockSpec((1, heads, SPAN), lambda b, i: (b, 0, 0)),
                by_block(heads),
                by_block(heads),
                pl.BlockSpec((1, 1, inner), lambda b, i: (b, 0, 0)),
                whole((1, inner)),
                whole((heads, inner)),
            ],
            out_specs=[by_block(inner), by_block(groups * state), whole((state, inner))],
            scratch_shapes=[
                pltpu.VMEM((SPAN + 8, inner), F32),
                pltpu.VMEM((SPAN + 8, maps), F32),
                pltpu.VMEM((state, inner), F32),
            ],
        ),
        out_shape=[
            jax.ShapeDtypeStruct((rows, inner), F32),
            jax.ShapeDtypeStruct((rows, groups * state), BF16),
            jax.ShapeDtypeStruct((state, inner), BF16),
        ],
        compiler_params=pltpu.CompilerParams(vmem_limit_bytes=lim),
        cost_estimate=pl.CostEstimate(flops=4_000_000_000, bytes_accessed=12_000_000, transcendentals=4_000_000),
        name="scan",
    )(
        index,
        *([x_got] * pieces),
        *([m_got] * pieces),
        rim_x,
        rim_m,
        conv_values,
        conv_maps.reshape(4, maps),
        marks,
        segment[:, None, :],
        cum.reshape(rows, heads),
        rev,
        carry.reshape(rows, heads),
        reach.reshape(rows, heads),
        gate_rows,
        jnp.repeat(skip_gain, width)[None, :],
        expand,
    )

    if lax.axis_size("ctx") == 2:
        arriving = passed_along(slab, "ctx", 1)
    else:
        slabs = lax.all_gather(slab, "ctx")
        factors = lax.all_gather(jnp.repeat(before[blocks], width), "ctx")

        def one(turn, total):
            return (
                lax.dynamic_index_in_dim(factors, turn, 0, False)[None, :] * total
                + lax.dynamic_index_in_dim(slabs, turn, 0, False).astype(F32)
            )

        arriving = lax.fori_loop(0, lax.axis_index("ctx"), one, jnp.zeros(slab.shape, F32)).astype(BF16)

    normed = pl.pallas_call(
        functools.partial(gate_kernel, pieces, groups, heads, state, width),
        grid_spec=pltpu.PrefetchScalarGridSpec(
            num_scalar_prefetch=1,
            grid=(blocks,),
            in_specs=piece_specs(inner)
            + [
                by_block(inner),
                by_block(groups * state),
                by_block(heads),
                whole((state, inner)),
                whole((heads, inner)),
                whole((1, inner)),
            ],
            out_specs=by_block(inner),
            scratch_shapes=[pltpu.VMEM((SPAN, inner // groups), F32), pltpu.VMEM((SPAN, inner), BF16)],
        ),
        out_shape=jax.ShapeDtypeStruct((rows, inner), BF16),
        compiler_params=pltpu.CompilerParams(vmem_limit_bytes=lim),
        cost_estimate=pl.CostEstimate(flops=1_000_000_000, bytes_accessed=10_000_000, transcendentals=1_000_000),
        name="gating",
    )(
        index,
        *([z_got] * pieces),
        y_part,
        c_all,
        coef.reshape(rows, heads),
        arriving,
        expand,
        norm_gain[None, :],
    )
    partial_value = jnp.dot(normed, out_weight, preferred_element_type=F32)
    result = lax.psum_scatter(partial_value.astype(BF16), "head", scatter_dimension=1, tiled=True)
    return result[None]


def solution(mesh):
    return jax.shard_map(
        body,
        mesh=mesh,
        in_specs=(
            P("dp", "ctx", "head"),
            P("dp", "ctx", "head"),
            P("dp", "ctx", "head", None),
            P("dp", "ctx", "head"),
            P("head"),
            P("head"),
            P(None, "head"),
            P(None, "head", None),
            P(),
            P("dp", "ctx"),
            P("head"),
            P("head", None),
        ),
        out_specs=P("dp", "ctx", "head"),
        check_vma=False,
    )
```

```python
import functools

import jax
import jax.numpy as jnp
from jax import lax
from jax.experimental import pallas as pl
from jax.experimental.pallas import tpu as pltpu
from jax.sharding import PartitionSpec as P

SPAN = 128
eps = 1e-05
F32 = jnp.float32
BF16 = jnp.bfloat16


def silu(u):
    return u * (1.0 / (1.0 + jnp.exp(-u)))


def spread_heads(coef, expand):
    high = coef.astype(BF16)
    low = (coef - high.astype(F32)).astype(BF16)
    return jnp.dot(high, expand, preferred_element_type=F32) + jnp.dot(
        low, expand, preferred_element_type=F32
    )


def conv_cols(buf, cols, taps, marks):
    summed = taps[3:4, :] * buf[8 : 8 + SPAN, cols]
    for back in range(1, 4):
        keep = marks[:, 2 + back : 3 + back]
        summed = summed + (taps[3 - back : 4 - back, :] * buf[8 - back : 8 - back + SPAN, cols]) * keep
    return silu(summed).astype(BF16)


def scan_kernel(pieces, groups, heads, state, width, index_ref, *refs):
    x_refs = refs[:pieces]
    m_refs = refs[pieces : 2 * pieces]
    (rim_x, rim_m, taps_x, taps_m, marks_ref, segrow_ref, cum_ref, rev_ref, carry_ref, reach_ref,
     gate_ref, skip_ref, expand_ref, y_ref, c_ref, slab_ref, xbuf, mbuf, carried) = refs[2 * pieces :]
    block = pl.program_id(0)
    prow = SPAN // pieces
    inner = xbuf.shape[1]
    maps = mbuf.shape[1]

    @pl.when(block == 0)
    def _():
        xbuf[0:8, :] = rim_x[prow - 8 : prow, :].astype(F32)
        mbuf[0:8, :] = rim_m[prow - 8 : prow, :maps].astype(F32)
        carried[...] = jnp.zeros_like(carried)

    @pl.when(block > 0)
    def _():
        xbuf[0:8, :] = xbuf[SPAN : SPAN + 8, :]
        mbuf[0:8, :] = mbuf[SPAN : SPAN + 8, :]

    for k in range(pieces):
        xbuf[8 + k * prow : 8 + (k + 1) * prow, :] = x_refs[k][0].astype(F32)
        mbuf[8 + k * prow : 8 + (k + 1) * prow, :] = m_refs[k][0].astype(F32)
    marks = marks_ref[...]
    seg_t = marks[:, 0:1]
    ti = lax.broadcasted_iota(jnp.int32, (SPAN, SPAN), 0)
    si = lax.broadcasted_iota(jnp.int32, (SPAN, SPAN), 1)
    allowed = (ti >= si) & (seg_t == segrow_ref[0])
    bias = jnp.where(allowed, 0.0, -1e30)
    left = lax.broadcasted_iota(jnp.int32, (SPAN, 2 * width), 1) < width
    cum = cum_ref[...]
    rev = rev_ref[0]
    carry = carry_ref[...]
    reach = reach_ref[...]
    per_group = heads // groups
    for g in range(groups):
        parts = []
        for q in range(2 * state // 128):
            cols = slice(g * 2 * state + q * 128, g * 2 * state + (q + 1) * 128)
            parts.append(conv_cols(mbuf, cols, taps_m[:, cols], marks))
        half = len(parts) // 2
        b_g = jnp.concatenate(parts[:half], axis=1)
        c_g = jnp.concatenate(parts[half:], axis=1)
        c_ref[:, g * state : (g + 1) * state] = c_g
        scores = lax.dot_general(c_g, b_g, (((1,), (1,)), ((), ())), preferred_element_type=F32)
        for p in range(per_group // 2):
            h = g * per_group + 2 * p
            cols = slice(h * width, (h + 2) * width)
            xc = conv_cols(xbuf, cols, taps_x[:, cols], marks)
            weights = []
            for k in (h, h + 1):
                decay = jnp.exp((cum[:, k : k + 1] + rev[k : k + 1, :]) + bias)
                weights.append((decay * scores).astype(BF16))
            zero = jnp.zeros_like(xc)
            both = jnp.concatenate([jnp.where(left, xc, zero), jnp.where(left, zero, xc)], axis=0)
            y = jnp.dot(jnp.concatenate(weights, axis=1), both, preferred_element_type=F32)
            expand = expand_ref[:, cols]
            prior = carried[:, cols]
            off = jnp.dot(c_g, prior.astype(BF16), preferred_element_type=F32)
            xf = xc.astype(F32)
            y_ref[:, cols] = y + off * spread_heads(reach, expand) + skip_ref[:, cols] * xf
            xw = (xf * spread_heads(carry, expand)).astype(BF16)
            added = lax.dot_general(b_g, xw, (((0,), (0,)), ((), ())), preferred_element_type=F32)
            carried[:, cols] = gate_ref[0, :, cols] * prior + added

    @pl.when(block == pl.num_programs(0) - 1)
    def _():
        slab_ref[...] = carried[...].astype(BF16)


def gate_kernel(pieces, groups, heads, state, width, index_ref, *refs):
    z_refs = refs[:pieces]
    y_ref, c_ref, coef_ref, arriving_ref, expand_ref, gain_ref, out_ref, gated, zbuf = refs[pieces:]
    prow = SPAN // pieces
    for k in range(pieces):
        zbuf[k * prow : (k + 1) * prow, :] = z_refs[k][0]
    coef = coef_ref[...]
    inner = heads * width
    size = inner // groups
    for g in range(groups):
        c_g = c_ref[:, g * state : (g + 1) * state]
        total = jnp.zeros((SPAN, 128), F32)
        for q in range(size // 128):
            cols = slice(g * size + q * 128, g * size + (q + 1) * 128)
            off = jnp.dot(c_g, arriving_ref[:, cols], preferred_element_type=F32)
            y = y_ref[:, cols] + off * spread_heads(coef, expand_ref[:, cols])
            value = y * silu(zbuf[:, cols].astype(F32))
            gated[:, q * 128 : (q + 1) * 128] = value
            total = total + value * value
        scale = lax.rsqrt(jnp.sum(total, axis=1, keepdims=True) * (1.0 / size) + eps)
        for q in range(size // 128):
            cols = slice(g * size + q * 128, g * size + (q + 1) * 128)
            out_ref[:, cols] = (
                gated[:, q * 128 : (q + 1) * 128] * scale * gain_ref[:, cols]
            ).astype(BF16)


def passed_along(block, axis, distance):
    devices = range(lax.axis_size(axis))
    route = [(i - distance, i) for i in devices if i - distance in devices]
    return lax.ppermute(block, axis, route)


def body(token_values, gate_values, state_maps, step_raw, log_rate, skip_gain, conv_values, conv_maps,
         piece_shift, doc_start, norm_gain, out_weight):
    owners = lax.axis_size(("dp", "ctx"))
    myself = lax.axis_index(("dp", "ctx"))
    slots = piece_shift.shape[0]
    rows = token_values.shape[1]
    prow = rows // slots
    most = 2 * slots // owners
    inner = token_values.shape[2]
    heads = log_rate.shape[0]
    groups = state_maps.shape[2]
    state = state_maps.shape[3] // 2
    maps = groups * 2 * state
    width = inner // heads
    blocks = rows // SPAN
    pieces = SPAN // prow

    slot_ids = jnp.arange(slots, dtype=jnp.int32)
    matching = piece_shift[:, None] == piece_shift[None, :]
    ranking = jnp.sum((matching & (slot_ids[None, :] < slot_ids[:, None])).astype(jnp.int32), axis=1)
    base = most // 2 if owners <= 8 else most
    offsets = (jnp.arange(owners, dtype=jnp.int32) - myself) % owners
    chosen = (piece_shift[None, None, :] == offsets[:, None, None]) & (
        ranking[None, None, :] == jnp.arange(base, dtype=jnp.int32)[None, :, None]
    )
    send_slot = jnp.sum(chosen.astype(jnp.int32) * slot_ids[None, None, :], axis=2)
    source = (myself - piece_shift) % owners
    index = source * base + ranking

    def exchange(cut):
        got = lax.all_to_all(cut[send_slot], ("dp", "ctx"), split_axis=0, concat_axis=0, tiled=True)
        return got.reshape((owners * base,) + cut.shape[1:])

    steps = jnp.pad(step_raw[0], ((0, 0), (0, (-heads) % 128)))
    x_cut = jnp.concatenate(
        [token_values[0], state_maps[0].reshape(rows, maps), steps], axis=1
    ).reshape(slots, prow, -1)
    z_cut = gate_values[0].reshape(slots, prow, inner)
    cuts = (x_cut, z_cut)
    if base < most:
        shifts = jnp.arange(owners, dtype=jnp.int32)
        counts = jnp.sum((piece_shift[None, :] == shifts[:, None]).astype(jnp.int32), axis=1)
        over = (counts > base).astype(jnp.int32)
        place = jnp.sum(over[None, :] * (shifts[None, :] < shifts[:, None]), axis=1)
        spare = slots // (base + 1)
        nth = over[None, :] * (place[None, :] == jnp.arange(spare)[:, None])
        shift_of = jnp.sum(nth * shifts[None, :], axis=1)
        surplus = jnp.sum(nth * (counts - base)[None, :], axis=1)
        late = (piece_shift[None, None, :] == shift_of[:, None, None]) & (
            ranking[None, None, :] == base + jnp.arange(most - base, dtype=jnp.int32)[None, :, None]
        )
        late_slot = jnp.sum(late.astype(jnp.int32) * slot_ids[None, None, :], axis=2)
        mine = jnp.sum((piece_shift[:, None] == shifts[None, :]) * place[None, :], axis=1)
        index = jnp.where(
            ranking < base, index, owners * base + mine * (most - base) + ranking - base
        )

        def moving(shift, number):
            def move(ids, cuts):
                out = []
                for cut in cuts:
                    part = cut[ids[:number]]
                    if shift:
                        part = lax.ppermute(
                            part, ("dp", "ctx"), [(t, (t + shift) % owners) for t in range(owners)]
                        )
                    out.append(jnp.pad(part, ((0, most - base - number), (0, 0), (0, 0))))
                return tuple(out)

            return move

        which = shift_of * (most - base) + surplus - 1
        moves = [moving(s, n) for s in range(owners) for n in range(1, most - base + 1)]

        def one_shift(turn, held):
            parts = lax.switch(which[turn], moves, late_slot[turn], cuts)
            return tuple(
                lax.dynamic_update_slice_in_dim(h, p, turn * (most - base), 0)
                for h, p in zip(held, parts)
            )

        held = tuple(jnp.zeros((spare * (most - base),) + cut.shape[1:], cut.dtype) for cut in cuts)
        held = lax.fori_loop(0, jnp.sum(over), one_shift, held)
        x_got = jnp.concatenate([exchange(x_cut), held[0]])
        z_sent, z_held = lax.optimization_barrier((z_cut[send_slot], held[1]))
        z_got = lax.all_to_all(z_sent, ("dp", "ctx"), split_axis=0, concat_axis=0, tiled=True)
        z_got = jnp.concatenate([z_got.reshape((owners * base, prow, inner)), z_held])
    else:
        x_got, z_got = (exchange(cut) for cut in cuts)

    flags = doc_start[0].astype(F32)
    tail = passed_along(flags[rows - 3 :], "ctx", 1)
    free = 1.0 - jnp.concatenate([tail, flags])
    k1 = free[3:]
    k2 = k1 * free[2 : 2 + rows]
    k3 = k2 * free[1 : 1 + rows]
    segment = jnp.cumsum(flags.reshape(blocks, SPAN), axis=1)
    same_end = (segment == segment[:, -1:]).astype(F32)
    first = (segment == 0).astype(F32)
    nil = jnp.zeros((rows,), F32)
    marks = jnp.stack(
        [segment.reshape(rows), same_end.reshape(rows), first.reshape(rows), k1, k2, k3, nil, nil], axis=1
    )

    dt_raw = x_got[:, :, inner + maps : inner + maps + heads][index].reshape(rows, heads)
    dt = jax.nn.softplus(dt_raw.astype(F32)).reshape(blocks, SPAN, heads)
    cum = jnp.cumsum(dt * (-jnp.exp(log_rate)), axis=1)
    rev = (jnp.log(dt) - cum).transpose(0, 2, 1)
    last = cum[:, -1:]
    carry = jnp.exp(last - cum) * dt * same_end[:, :, None]
    reach = jnp.exp(cum) * first[:, :, None]
    gates = jnp.exp(cum[:, -1]) * first[:, -1:]
    before = [jnp.ones((heads,), F32)]
    for b in range(blocks):
        before.append(before[-1] * gates[b])
    coef = reach * jnp.stack(before[:blocks])[:, None, :]
    gate_rows = jnp.repeat(gates, width, axis=1)[:, None, :]
    expand = (
        jnp.arange(heads)[:, None] == jnp.arange(inner)[None, :] // width
    ).astype(BF16)

    rim = passed_along(x_got[index[slots - 1]], "ctx", 1)
    rim_x, rim_m = rim[:, :inner], rim[:, inner : inner + maps]

    def piece_specs(cols, at=0):
        return [
            pl.BlockSpec((1, prow, cols), functools.partial(lambda k, b, i: (i[b * pieces + k], 0, at), k))
            for k in range(pieces)
        ]

    def whole(shape):
        return pl.BlockSpec(shape, lambda b, i: (0,) * len(shape))

    def by_block(cols):
        return pl.BlockSpec((SPAN, cols), lambda b, i: (b, 0))

    lim = 48 * 1024 * 1024
    y_part, c_all, slab = pl.pallas_call(
        functools.partial(scan_kernel, pieces, groups, heads, state, width),
        grid_spec=pltpu.PrefetchScalarGridSpec(
            num_scalar_prefetch=1,
            grid=(blocks,),
            in_specs=piece_specs(inner)
            + piece_specs(maps, inner // maps)
            + [
                whole((prow, inner)),
                whole(rim_m.shape),
                whole((4, inner)),
                whole((4, maps)),
                by_block(8),
                pl.BlockSpec((1, 1, SPAN), lambda b, i: (b, 0, 0)),
                by_block(heads),
                pl.BlockSpec((1, heads, SPAN), lambda b, i: (b, 0, 0)),
                by_block(heads),
                by_block(heads),
                pl.BlockSpec((1, 1, inner), lambda b, i: (b, 0, 0)),
                whole((1, inner)),
                whole((heads, inner)),
            ],
            out_specs=[by_block(inner), by_block(groups * state), whole((state, inner))],
            scratch_shapes=[
                pltpu.VMEM((SPAN + 8, inner), F32),
                pltpu.VMEM((SPAN + 8, maps), F32),
                pltpu.VMEM((state, inner), F32),
            ],
        ),
        out_shape=[
            jax.ShapeDtypeStruct((rows, inner), F32),
            jax.ShapeDtypeStruct((rows, groups * state), BF16),
            jax.ShapeDtypeStruct((state, inner), BF16),
        ],
        compiler_params=pltpu.CompilerParams(vmem_limit_bytes=lim),
        cost_estimate=pl.CostEstimate(flops=4_000_000_000, bytes_accessed=12_000_000, transcendentals=4_000_000),
        name="scan",
    )(
        index,
        *([x_got] * pieces),
        *([x_got] * pieces),
        rim_x,
        rim_m,
        conv_values,
        conv_maps.reshape(4, maps),
        marks,
        segment[:, None, :],
        cum.reshape(rows, heads),
        rev,
        carry.reshape(rows, heads),
        reach.reshape(rows, heads),
        gate_rows,
        jnp.repeat(skip_gain, width)[None, :],
        expand,
    )

    if lax.axis_size("ctx") == 2:
        arriving = passed_along(slab, "ctx", 1)
    else:
        slabs = lax.all_gather(slab, "ctx")
        factors = lax.all_gather(jnp.repeat(before[blocks], width), "ctx")

        def one(turn, total):
            return (
                lax.dynamic_index_in_dim(factors, turn, 0, False)[None, :] * total
                + lax.dynamic_index_in_dim(slabs, turn, 0, False).astype(F32)
            )

        arriving = lax.fori_loop(0, lax.axis_index("ctx"), one, jnp.zeros(slab.shape, F32)).astype(BF16)

    normed = pl.pallas_call(
        functools.partial(gate_kernel, pieces, groups, heads, state, width),
        grid_spec=pltpu.PrefetchScalarGridSpec(
            num_scalar_prefetch=1,
            grid=(blocks,),
            in_specs=piece_specs(inner)
            + [
                by_block(inner),
                by_block(groups * state),
                by_block(heads),
                whole((state, inner)),
                whole((heads, inner)),
                whole((1, inner)),
            ],
            out_specs=by_block(inner),
            scratch_shapes=[pltpu.VMEM((SPAN, inner // groups), F32), pltpu.VMEM((SPAN, inner), BF16)],
        ),
        out_shape=jax.ShapeDtypeStruct((rows, inner), BF16),
        compiler_params=pltpu.CompilerParams(vmem_limit_bytes=lim),
        cost_estimate=pl.CostEstimate(flops=1_000_000_000, bytes_accessed=10_000_000, transcendentals=1_000_000),
        name="gating",
    )(
        index,
        *([z_got] * pieces),
        y_part,
        c_all,
        coef.reshape(rows, heads),
        arriving,
        expand,
        norm_gain[None, :],
    )
    partial_value = jnp.dot(normed, out_weight, preferred_element_type=F32)
    result = lax.psum_scatter(partial_value.astype(BF16), "head", scatter_dimension=1, tiled=True)
    return result[None]


def solution(mesh):
    return jax.shard_map(
        body,
        mesh=mesh,
        in_specs=(
            P("dp", "ctx", "head"),
            P("dp", "ctx", "head"),
            P("dp", "ctx", "head", None),
            P("dp", "ctx", "head"),
            P("head"),
            P("head"),
            P(None, "head"),
            P(None, "head", None),
            P(),
            P("dp", "ctx"),
            P("head"),
            P("head", None),
        ),
        out_specs=P("dp", "ctx", "head"),
        check_vma=False,
    )
```

```python
import functools

import jax
import jax.numpy as jnp
from jax import lax
from jax.experimental import pallas as pl
from jax.experimental.pallas import tpu as pltpu
from jax.sharding import PartitionSpec as P

SPAN = 128
eps = 1e-05
F32 = jnp.float32
BF16 = jnp.bfloat16


def silu(u):
    return u * (1.0 / (1.0 + jnp.exp(-u)))


def spread_heads(coef, expand):
    high = coef.astype(BF16)
    low = (coef - high.astype(F32)).astype(BF16)
    return jnp.dot(high, expand, preferred_element_type=F32) + jnp.dot(
        low, expand, preferred_element_type=F32
    )


def conv_cols(buf, cols, taps, marks):
    summed = taps[3:4, :] * buf[8 : 8 + SPAN, cols]
    for back in range(1, 4):
        keep = marks[:, 2 + back : 3 + back]
        summed = summed + (taps[3 - back : 4 - back, :] * buf[8 - back : 8 - back + SPAN, cols]) * keep
    return silu(summed).astype(BF16)


def scan_kernel(pieces, groups, heads, state, width, index_ref, *refs):
    x_refs = refs[:pieces]
    m_refs = refs[pieces : 2 * pieces]
    (rim_x, rim_m, taps_x, taps_m, marks_ref, segrow_ref, cum_ref, rev_ref, carry_ref, reach_ref,
     gate_ref, skip_ref, expand_ref, y_ref, c_ref, slab_ref, xbuf, mbuf, carried) = refs[2 * pieces :]
    block = pl.program_id(0)
    prow = SPAN // pieces
    inner = xbuf.shape[1]
    maps = mbuf.shape[1]

    @pl.when(block == 0)
    def _():
        xbuf[0:8, :] = rim_x[prow - 8 : prow, :].astype(F32)
        mbuf[0:8, :] = rim_m[prow - 8 : prow, :maps].astype(F32)
        carried[...] = jnp.zeros_like(carried)

    @pl.when(block > 0)
    def _():
        xbuf[0:8, :] = xbuf[SPAN : SPAN + 8, :]
        mbuf[0:8, :] = mbuf[SPAN : SPAN + 8, :]

    for k in range(pieces):
        xbuf[8 + k * prow : 8 + (k + 1) * prow, :] = x_refs[k][0].astype(F32)
        mbuf[8 + k * prow : 8 + (k + 1) * prow, :] = m_refs[k][0].astype(F32)
    marks = marks_ref[...]
    seg_t = marks[:, 0:1]
    ti = lax.broadcasted_iota(jnp.int32, (SPAN, SPAN), 0)
    si = lax.broadcasted_iota(jnp.int32, (SPAN, SPAN), 1)
    allowed = (ti >= si) & (seg_t == segrow_ref[0])
    bias = jnp.where(allowed, 0.0, -1e30)
    left = lax.broadcasted_iota(jnp.int32, (SPAN, 2 * width), 1) < width
    cum = cum_ref[...]
    rev = rev_ref[0]
    carry = carry_ref[...]
    reach = reach_ref[...]
    per_group = heads // groups
    for g in range(groups):
        parts = []
        for q in range(2 * state // 128):
            cols = slice(g * 2 * state + q * 128, g * 2 * state + (q + 1) * 128)
            parts.append(conv_cols(mbuf, cols, taps_m[:, cols], marks))
        half = len(parts) // 2
        b_g = jnp.concatenate(parts[:half], axis=1)
        c_g = jnp.concatenate(parts[half:], axis=1)
        c_ref[:, g * state : (g + 1) * state] = c_g
        scores = lax.dot_general(c_g, b_g, (((1,), (1,)), ((), ())), preferred_element_type=F32)
        for p in range(per_group // 2):
            h = g * per_group + 2 * p
            cols = slice(h * width, (h + 2) * width)
            xc = conv_cols(xbuf, cols, taps_x[:, cols], marks)
            weights = []
            for k in (h, h + 1):
                decay = jnp.exp((cum[:, k : k + 1] + rev[k : k + 1, :]) + bias)
                weights.append((decay * scores).astype(BF16))
            zero = jnp.zeros_like(xc)
            both = jnp.concatenate([jnp.where(left, xc, zero), jnp.where(left, zero, xc)], axis=0)
            y = jnp.dot(jnp.concatenate(weights, axis=1), both, preferred_element_type=F32)
            expand = expand_ref[:, cols]
            prior = carried[:, cols]
            off = jnp.dot(c_g, prior.astype(BF16), preferred_element_type=F32)
            xf = xc.astype(F32)
            y_ref[:, cols] = y + off * spread_heads(reach, expand) + skip_ref[:, cols] * xf
            xw = (xf * spread_heads(carry, expand)).astype(BF16)
            added = lax.dot_general(b_g, xw, (((0,), (0,)), ((), ())), preferred_element_type=F32)
            carried[:, cols] = gate_ref[0, :, cols] * prior + added

    @pl.when(block == pl.num_programs(0) - 1)
    def _():
        slab_ref[...] = carried[...].astype(BF16)


def gate_kernel(pieces, groups, heads, state, width, index_ref, *refs):
    z_refs = refs[:pieces]
    y_ref, c_ref, coef_ref, arriving_ref, expand_ref, gain_ref, out_ref, gated, zbuf = refs[pieces:]
    prow = SPAN // pieces
    for k in range(pieces):
        zbuf[k * prow : (k + 1) * prow, :] = z_refs[k][0]
    coef = coef_ref[...]
    inner = heads * width
    size = inner // groups
    for g in range(groups):
        c_g = c_ref[:, g * state : (g + 1) * state]
        total = jnp.zeros((SPAN, 128), F32)
        for q in range(size // 128):
            cols = slice(g * size + q * 128, g * size + (q + 1) * 128)
            off = jnp.dot(c_g, arriving_ref[:, cols], preferred_element_type=F32)
            y = y_ref[:, cols] + off * spread_heads(coef, expand_ref[:, cols])
            value = y * silu(zbuf[:, cols].astype(F32))
            gated[:, q * 128 : (q + 1) * 128] = value
            total = total + value * value
        scale = lax.rsqrt(jnp.sum(total, axis=1, keepdims=True) * (1.0 / size) + eps)
        for q in range(size // 128):
            cols = slice(g * size + q * 128, g * size + (q + 1) * 128)
            out_ref[:, cols] = (
                gated[:, q * 128 : (q + 1) * 128] * scale * gain_ref[:, cols]
            ).astype(BF16)


def project_kernel(n, cuts, a_ref, w_ref, out_ref, send, from_left, from_right, total, send_sem, left_sem, right_sem):
    me = lax.axis_index("head")
    tall = out_ref.shape[0] // cuts
    wide = out_ref.shape[1]
    tile = 256
    mesh_ids = pl.DeviceIdType.MESH
    right = lax.rem(me + 1, n)
    left = lax.rem(me + n - 1, n)
    has_left = me > 0
    has_right = me < n - 1
    barrier = pltpu.get_barrier_semaphore()

    @pl.when(has_left)
    def _():
        pl.semaphore_signal(barrier, inc=1, device_id={"head": left}, device_id_type=mesh_ids)

    @pl.when(has_right)
    def _():
        pl.semaphore_signal(barrier, inc=1, device_id={"head": right}, device_id_type=mesh_ids)

    pl.semaphore_wait(barrier, jnp.where(has_left & has_right, 2, 1))

    def rightward(place):
        return pltpu.make_async_remote_copy(
            src_ref=send.at[place], dst_ref=from_left.at[place], send_sem=send_sem.at[place],
            recv_sem=left_sem.at[place], device_id={"head": right}, device_id_type=mesh_ids)

    def leftward(place):
        return pltpu.make_async_remote_copy(
            src_ref=send.at[place], dst_ref=from_right.at[place], send_sem=send_sem.at[place],
            recv_sem=right_sem.at[place], device_id={"head": left}, device_id_type=mesh_ids)

    def product(chunk, cut):
        rows = a_ref[pl.ds(pl.multiple_of(cut * tall, tall), tall), :]
        for q in range(wide // tile):
            cols = pl.ds(pl.multiple_of(chunk * wide + q * tile, tile), tile)
            total[:, q * tile : (q + 1) * tile] = jnp.dot(rows, w_ref[:, cols], preferred_element_type=F32)

    def step(turn, carry):
        cut = lax.rem(turn, cuts)
        up = n - 1 - turn // cuts
        down = turn // cuts

        @pl.when(me < up)
        def _():
            place = up * cuts + cut
            product(up, cut)

            @pl.when(has_left)
            def _():
                rightward(place).wait_recv()
                total[...] += from_left[place].astype(F32)

            send[place] = total[...].astype(BF16)
            rightward(place).start()

        @pl.when(me > down)
        def _():
            place = down * cuts + cut
            product(down, cut)

            @pl.when(has_right)
            def _():
                leftward(place).wait_recv()
                total[...] += from_right[place].astype(F32)

            send[place] = total[...].astype(BF16)
            leftward(place).start()

        return carry

    lax.fori_loop(0, (n - 1) * cuts, step, 0)

    def finish(cut, carry):
        place = me * cuts + cut
        product(me, cut)

        @pl.when(has_left)
        def _():
            rightward(place).wait_recv()
            total[...] += from_left[place].astype(F32)

        @pl.when(has_right)
        def _():
            leftward(place).wait_recv()
            total[...] += from_right[place].astype(F32)

        out_ref[pl.ds(pl.multiple_of(cut * tall, tall), tall), :] = total[...].astype(BF16)
        return carry

    lax.fori_loop(0, cuts, finish, 0)

    def drain(turn, carry):
        @pl.when(turn // cuts > me)
        def _():
            rightward(turn).wait_send()

        @pl.when(turn // cuts < me)
        def _():
            leftward(turn).wait_send()

        return carry

    lax.fori_loop(0, n * cuts, drain, 0)


def passed_along(block, axis, distance):
    devices = range(lax.axis_size(axis))
    route = [(i - distance, i) for i in devices if i - distance in devices]
    return lax.ppermute(block, axis, route)


def body(token_values, gate_values, state_maps, step_raw, log_rate, skip_gain, conv_values, conv_maps,
         piece_shift, doc_start, norm_gain, out_weight):
    owners = lax.axis_size(("dp", "ctx"))
    myself = lax.axis_index(("dp", "ctx"))
    slots = piece_shift.shape[0]
    rows = token_values.shape[1]
    prow = rows // slots
    most = 2 * slots // owners
    inner = token_values.shape[2]
    heads = log_rate.shape[0]
    groups = state_maps.shape[2]
    state = state_maps.shape[3] // 2
    maps = groups * 2 * state
    width = inner // heads
    blocks = rows // SPAN
    pieces = SPAN // prow

    slot_ids = jnp.arange(slots, dtype=jnp.int32)
    matching = piece_shift[:, None] == piece_shift[None, :]
    ranking = jnp.sum((matching & (slot_ids[None, :] < slot_ids[:, None])).astype(jnp.int32), axis=1)
    base = most // 2 if owners <= 8 else most
    offsets = (jnp.arange(owners, dtype=jnp.int32) - myself) % owners
    chosen = (piece_shift[None, None, :] == offsets[:, None, None]) & (
        ranking[None, None, :] == jnp.arange(base, dtype=jnp.int32)[None, :, None]
    )
    send_slot = jnp.sum(chosen.astype(jnp.int32) * slot_ids[None, None, :], axis=2)
    source = (myself - piece_shift) % owners
    index = source * base + ranking

    def exchange(cut):
        got = lax.all_to_all(cut[send_slot], ("dp", "ctx"), split_axis=0, concat_axis=0, tiled=True)
        return got.reshape((owners * base,) + cut.shape[1:])

    steps = jnp.pad(step_raw[0], ((0, 0), (0, (-heads) % 128)))
    x_cut = jnp.concatenate(
        [token_values[0], state_maps[0].reshape(rows, maps), steps], axis=1
    ).reshape(slots, prow, -1)
    z_cut = gate_values[0].reshape(slots, prow, inner)
    cuts = (x_cut, z_cut)
    if base < most:
        shifts = jnp.arange(owners, dtype=jnp.int32)
        counts = jnp.sum((piece_shift[None, :] == shifts[:, None]).astype(jnp.int32), axis=1)
        over = (counts > base).astype(jnp.int32)
        place = jnp.sum(over[None, :] * (shifts[None, :] < shifts[:, None]), axis=1)
        spare = slots // (base + 1)
        nth = over[None, :] * (place[None, :] == jnp.arange(spare)[:, None])
        shift_of = jnp.sum(nth * shifts[None, :], axis=1)
        surplus = jnp.sum(nth * (counts - base)[None, :], axis=1)
        late = (piece_shift[None, None, :] == shift_of[:, None, None]) & (
            ranking[None, None, :] == base + jnp.arange(most - base, dtype=jnp.int32)[None, :, None]
        )
        late_slot = jnp.sum(late.astype(jnp.int32) * slot_ids[None, None, :], axis=2)
        mine = jnp.sum((piece_shift[:, None] == shifts[None, :]) * place[None, :], axis=1)
        index = jnp.where(
            ranking < base, index, owners * base + mine * (most - base) + ranking - base
        )

        def moving(shift, number):
            def move(ids, cuts):
                out = []
                for cut in cuts:
                    part = cut[ids[:number]]
                    if shift:
                        part = lax.ppermute(
                            part, ("dp", "ctx"), [(t, (t + shift) % owners) for t in range(owners)]
                        )
                    out.append(jnp.pad(part, ((0, most - base - number), (0, 0), (0, 0))))
                return tuple(out)

            return move

        which = shift_of * (most - base) + surplus - 1
        moves = [moving(s, n) for s in range(owners) for n in range(1, most - base + 1)]

        def one_shift(turn, held):
            parts = lax.switch(which[turn], moves, late_slot[turn], cuts)
            return tuple(
                lax.dynamic_update_slice_in_dim(h, p, turn * (most - base), 0)
                for h, p in zip(held, parts)
            )

        held = tuple(jnp.zeros((spare * (most - base),) + cut.shape[1:], cut.dtype) for cut in cuts)
        held = lax.fori_loop(0, jnp.sum(over), one_shift, held)
        x_got = jnp.concatenate([exchange(x_cut), held[0]])
        z_sent, z_held = lax.optimization_barrier((z_cut[send_slot], held[1]))
        z_got = lax.all_to_all(z_sent, ("dp", "ctx"), split_axis=0, concat_axis=0, tiled=True)
        z_got = jnp.concatenate([z_got.reshape((owners * base, prow, inner)), z_held])
    else:
        x_got, z_got = (exchange(cut) for cut in cuts)

    flags = doc_start[0].astype(F32)
    tail = passed_along(flags[rows - 3 :], "ctx", 1)
    free = 1.0 - jnp.concatenate([tail, flags])
    k1 = free[3:]
    k2 = k1 * free[2 : 2 + rows]
    k3 = k2 * free[1 : 1 + rows]
    segment = jnp.cumsum(flags.reshape(blocks, SPAN), axis=1)
    same_end = (segment == segment[:, -1:]).astype(F32)
    first = (segment == 0).astype(F32)
    nil = jnp.zeros((rows,), F32)
    marks = jnp.stack(
        [segment.reshape(rows), same_end.reshape(rows), first.reshape(rows), k1, k2, k3, nil, nil], axis=1
    )

    dt_raw = x_got[:, :, inner + maps : inner + maps + heads][index].reshape(rows, heads)
    dt = jax.nn.softplus(dt_raw.astype(F32)).reshape(blocks, SPAN, heads)
    cum = jnp.cumsum(dt * (-jnp.exp(log_rate)), axis=1)
    rev = (jnp.log(dt) - cum).transpose(0, 2, 1)
    last = cum[:, -1:]
    carry = jnp.exp(last - cum) * dt * same_end[:, :, None]
    reach = jnp.exp(cum) * first[:, :, None]
    gates = jnp.exp(cum[:, -1]) * first[:, -1:]
    before = [jnp.ones((heads,), F32)]
    for b in range(blocks):
        before.append(before[-1] * gates[b])
    coef = reach * jnp.stack(before[:blocks])[:, None, :]
    gate_rows = jnp.repeat(gates, width, axis=1)[:, None, :]
    expand = (
        jnp.arange(heads)[:, None] == jnp.arange(inner)[None, :] // width
    ).astype(BF16)

    rim = passed_along(x_got[index[slots - 1]], "ctx", 1)
    rim_x, rim_m = rim[:, :inner], rim[:, inner : inner + maps]

    def piece_specs(cols, at=0):
        return [
            pl.BlockSpec((1, prow, cols), functools.partial(lambda k, b, i: (i[b * pieces + k], 0, at), k))
            for k in range(pieces)
        ]

    def whole(shape):
        return pl.BlockSpec(shape, lambda b, i: (0,) * len(shape))

    def by_block(cols):
        return pl.BlockSpec((SPAN, cols), lambda b, i: (b, 0))

    lim = 48 * 1024 * 1024
    y_part, c_all, slab = pl.pallas_call(
        functools.partial(scan_kernel, pieces, groups, heads, state, width),
        grid_spec=pltpu.PrefetchScalarGridSpec(
            num_scalar_prefetch=1,
            grid=(blocks,),
            in_specs=piece_specs(inner)
            + piece_specs(maps, inner // maps)
            + [
                whole((prow, inner)),
                whole(rim_m.shape),
                whole((4, inner)),
                whole((4, maps)),
                by_block(8),
                pl.BlockSpec((1, 1, SPAN), lambda b, i: (b, 0, 0)),
                by_block(heads),
                pl.BlockSpec((1, heads, SPAN), lambda b, i: (b, 0, 0)),
                by_block(heads),
                by_block(heads),
                pl.BlockSpec((1, 1, inner), lambda b, i: (b, 0, 0)),
                whole((1, inner)),
                whole((heads, inner)),
            ],
            out_specs=[by_block(inner), by_block(groups * state), whole((state, inner))],
            scratch_shapes=[
                pltpu.VMEM((SPAN + 8, inner), F32),
                pltpu.VMEM((SPAN + 8, maps), F32),
                pltpu.VMEM((state, inner), F32),
            ],
        ),
        out_shape=[
            jax.ShapeDtypeStruct((rows, inner), F32),
            jax.ShapeDtypeStruct((rows, groups * state), BF16),
            jax.ShapeDtypeStruct((state, inner), BF16),
        ],
        compiler_params=pltpu.CompilerParams(vmem_limit_bytes=lim),
        cost_estimate=pl.CostEstimate(flops=4_000_000_000, bytes_accessed=12_000_000, transcendentals=4_000_000),
        name="scan",
    )(
        index,
        *([x_got] * pieces),
        *([x_got] * pieces),
        rim_x,
        rim_m,
        conv_values,
        conv_maps.reshape(4, maps),
        marks,
        segment[:, None, :],
        cum.reshape(rows, heads),
        rev,
        carry.reshape(rows, heads),
        reach.reshape(rows, heads),
        gate_rows,
        jnp.repeat(skip_gain, width)[None, :],
        expand,
    )

    if lax.axis_size("ctx") == 2:
        arriving = passed_along(slab, "ctx", 1)
    else:
        slabs = lax.all_gather(slab, "ctx")
        factors = lax.all_gather(jnp.repeat(before[blocks], width), "ctx")

        def one(turn, total):
            return (
                lax.dynamic_index_in_dim(factors, turn, 0, False)[None, :] * total
                + lax.dynamic_index_in_dim(slabs, turn, 0, False).astype(F32)
            )

        arriving = lax.fori_loop(0, lax.axis_index("ctx"), one, jnp.zeros(slab.shape, F32)).astype(BF16)

    normed = pl.pallas_call(
        functools.partial(gate_kernel, pieces, groups, heads, state, width),
        grid_spec=pltpu.PrefetchScalarGridSpec(
            num_scalar_prefetch=1,
            grid=(blocks,),
            in_specs=piece_specs(inner)
            + [
                by_block(inner),
                by_block(groups * state),
                by_block(heads),
                whole((state, inner)),
                whole((heads, inner)),
                whole((1, inner)),
            ],
            out_specs=by_block(inner),
            scratch_shapes=[pltpu.VMEM((SPAN, inner // groups), F32), pltpu.VMEM((SPAN, inner), BF16)],
        ),
        out_shape=jax.ShapeDtypeStruct((rows, inner), BF16),
        compiler_params=pltpu.CompilerParams(vmem_limit_bytes=lim),
        cost_estimate=pl.CostEstimate(flops=1_000_000_000, bytes_accessed=10_000_000, transcendentals=1_000_000),
        name="gating",
    )(
        index,
        *([z_got] * pieces),
        y_part,
        c_all,
        coef.reshape(rows, heads),
        arriving,
        expand,
        norm_gain[None, :],
    )
    n = lax.axis_size("head")
    cuts = 4
    wide = out_weight.shape[1] // n
    vmem = pl.BlockSpec(memory_space=pltpu.VMEM)
    held_shape = (n * cuts, rows // cuts, wide)
    result = pl.pallas_call(
        functools.partial(project_kernel, n, cuts),
        in_specs=[vmem, vmem],
        out_specs=vmem,
        out_shape=jax.ShapeDtypeStruct((rows, wide), BF16),
        scratch_shapes=[
            pltpu.VMEM(held_shape, BF16),
            pltpu.VMEM(held_shape, BF16),
            pltpu.VMEM(held_shape, BF16),
            pltpu.VMEM((rows // cuts, wide), F32),
            pltpu.SemaphoreType.DMA((n * cuts,)),
            pltpu.SemaphoreType.DMA((n * cuts,)),
            pltpu.SemaphoreType.DMA((n * cuts,)),
        ],
        compiler_params=pltpu.CompilerParams(collective_id=0, has_side_effects=True, vmem_limit_bytes=lim),
        cost_estimate=pl.CostEstimate(flops=9_000_000_000, bytes_accessed=20_000_000, transcendentals=0),
        name="project",
    )(normed, out_weight)
    return result[None]


def solution(mesh):
    return jax.shard_map(
        body,
        mesh=mesh,
        in_specs=(
            P("dp", "ctx", "head"),
            P("dp", "ctx", "head"),
            P("dp", "ctx", "head", None),
            P("dp", "ctx", "head"),
            P("head"),
            P("head"),
            P(None, "head"),
            P(None, "head", None),
            P(),
            P("dp", "ctx"),
            P("head"),
            P("head", None),
        ),
        out_specs=P("dp", "ctx", "head"),
        check_vma=False,
    )
```
